32 devices in a mesh: groups: 2 (over x), lon: 16 (over z, y, core).
Axes of the slice: x: 2, y: 2, z: 4, core: 2. Of those that a mesh axis runs over, the one named last changes fastest.
Arguments:
- state_in: bfloat16 [128, 768, 256], P('groups', 'lon'), parts along dimension 0, may hold values from -6 to 6
- target: bfloat16 [128, 768, 256], P('groups', 'lon'), parts along dimension 0, may hold values from -6 to 6
- ocean_mask: int32 [128, 768], P('groups', 'lon'), parts along dimension 0, may hold values from 0 to 1, as said below
- kernel_one: bfloat16 [3, 3, 256, 256], replicated, may hold values from -0.125 to 0.125
- kernel_two: bfloat16 [3, 3, 256, 256], replicated, may hold values from -0.125 to 0.125
Outputs:
- prediction: bfloat16 [128, 768, 256], P('groups', 'lon'), parts along dimension 0
- grad_one: float32 [6, 3, 256, 256], P('groups'), parts along dimension 0
- grad_two: float32 [6, 3, 256, 256], P('groups'), parts along dimension 0
The draws below stay inside these ranges and needn't reach their ends.
There are 2 independent parts, one for each index of `groups`. The reference program is written for one: setup_inputs(seed, part) draws one part's arguments, and reference() takes and returns one part's arrays. A program takes and returns all parts, laid end to end along the dimension named above; an argument that names none is the same for every part. Nothing has to cross between parts.
Inputs may be any that keep to these rules, and one draw needn't show every extreme that they name: `ocean_mask`: 1 marks an ocean cell and 0 a land cell.
All inputs are finite; a program needn't handle non-finite values.
Results may differ from the reference program's by a relative error of at most 0.02.
Values may be sent and summed in bfloat16 or wider, within the bound.
A program may use at most 192 MiB of HBM per device.

```python
import math
import jax
import jax.numpy as jnp
from jax import lax

C = 256
LAT = 64
NLON = 768


def draw_ocean_mask(key, part):
    first_key, second_key = jax.random.split(jax.random.fold_in(key, 11))
    coast = jax.random.randint(first_key, (NLON,), 0, 3 * LAT // 4)
    islands = jax.random.randint(second_key, (LAT, NLON), 0, 6)
    rows = lax.broadcasted_iota(jnp.int32, (LAT, NLON), 0)
    return ((rows >= coast[None, :]) & (islands != 0)).astype(jnp.int32)


def block_levels(own_key, extent, shards, low, high):
    loudness = 1.0
    for axis_at, parts in shards:
        draws = jax.random.uniform(jax.random.fold_in(jax.random.fold_in(own_key, 6), axis_at), (parts,), jnp.float32, low / len(shards), high / len(shards))
        loudness = loudness * jnp.repeat(jnp.exp(draws), extent[axis_at] // parts).reshape((-1,) + (1,) * (len(extent) - 1 - axis_at))
    return loudness


def normal_values(own_key, dims, scale, reach, shards=(), held_as=jnp.bfloat16):
    result = jax.random.normal(own_key, dims, jnp.float32) * scale
    if len(shards) > 0:
        result = block_levels(own_key, dims, shards, -0.22, 0.18) * result
    return jnp.clip(result, min=-reach, max=reach).astype(held_as)


def setup_inputs(seed: int = 0, part: int = 0) -> dict:
    key_list = jax.random.split(jax.random.key(seed), 6)
    part_splits = jax.random.split(jax.random.fold_in(key_list[5], part), 6)
    return {
        "state_in": normal_values(part_splits[0], (LAT, NLON, C), 1.0, 6.0, ((1, 16),)),
        "target": normal_values(part_splits[1], (LAT, NLON, C), 1.0, 6.0, ((1, 16),)),
        "ocean_mask": draw_ocean_mask(jax.random.fold_in(jax.random.fold_in(key_list[5], part), 71), part),
        "kernel_one": normal_values(key_list[3], (3, 3, C, C), (9 * C) ** -0.5, 0.125),
        "kernel_two": normal_values(key_list[4], (3, 3, C, C), (9 * C) ** -0.5, 0.125),
    }


def extend(values_in):
    wrapped = jnp.concatenate([values_in[:, -1:], values_in, values_in[:, :1]], axis=1)
    return jnp.concatenate([jnp.zeros_like(wrapped[:1]), wrapped, wrapped[-1:, ::-1]], axis=0)

def convolve(padded, kernel):
    height = padded.shape[0] - 2
    width = padded.shape[1] - 2
    channels = padded.shape[2]
    total = jnp.zeros((height * width, kernel.shape[3]), jnp.float32)
    for a in range(3):
        for b in range(3):
            piece = padded[a:a + height, b:b + width].reshape(height * width, channels)
            total = total + jnp.dot(piece, kernel[a, b], preferred_element_type=jnp.float32, precision=lax.Precision.HIGHEST)
    return total.reshape(height, width, kernel.shape[3])

def kernel_grad(padded, error_map):
    height = padded.shape[0] - 2
    width = padded.shape[1] - 2
    channels = padded.shape[2]
    flat_error = error_map.reshape(height * width, channels)
    blocks = []
    for a in range(3):
        for b in range(3):
            piece = padded[a:a + height, b:b + width].reshape(height * width, channels)
            blocks.append(lax.dot_general(piece, flat_error, (((0,), (0,)), ((), ())), preferred_element_type=jnp.float32))
    return jnp.stack(blocks).reshape(3, 3, channels, flat_error.shape[1])

def gelu_value(u):
    return u * 0.5 * (1.0 + jax.scipy.special.erf(u / math.sqrt(2.0)))

def gelu_slope(u):
    return 0.5 * (1.0 + jax.scipy.special.erf(u / math.sqrt(2.0))) + u * jnp.exp(-0.5 * u * u) / math.sqrt(2.0 * math.pi)

def reference(state_in, target, ocean_mask, kernel_one, kernel_two):
    is_ocean = ocean_mask[..., None] == 1
    oceanic = ocean_mask[..., None].astype(jnp.float32)
    masked = jnp.where(is_ocean, state_in, jnp.zeros_like(state_in))
    padded_one = extend(masked)
    pre_act = convolve(padded_one, kernel_one).astype(jnp.bfloat16)
    pre_value = pre_act.astype(jnp.float32)
    hidden = (gelu_value(pre_value) * oceanic).astype(jnp.bfloat16)
    padded_two = extend(hidden)
    output = convolve(padded_two, kernel_two)
    prediction = (output * oceanic).astype(jnp.bfloat16)
    error_scale = 1.0 / math.sqrt(LAT * NLON)
    error_map = (oceanic * (output - target.astype(jnp.float32)) * error_scale).astype(jnp.bfloat16)
    grad_two = kernel_grad(padded_two, error_map)
    kernel_wide = kernel_two.astype(jnp.float32)
    unused, pullback = jax.vjp(lambda hidden_wide: convolve(extend(hidden_wide), kernel_wide), hidden.astype(jnp.float32))
    hidden_grad = pullback(error_map.astype(jnp.float32))[0]
    pre_grad = (hidden_grad * gelu_slope(pre_value) * oceanic).astype(jnp.bfloat16)
    grad_one = kernel_grad(padded_one, pre_grad)
    return (prediction, grad_one, grad_two)
```

```python
import functools
import math

import jax
import jax.numpy as jnp
from jax import lax
from jax.experimental import pallas as pl
from jax.experimental.pallas import tpu as pltpu
from jax.sharding import PartitionSpec as P

F32, BF16 = jnp.float32, jnp.bfloat16
MESH = pl.DeviceIdType.MESH
ROWS = 8


def padded_rows(count, total):
    unit = 16 * count
    return -(-total // unit) * unit


def bit_orders(count):
    bits = list(range(count.bit_length() - 1))
    return bits, bits[:1] + bits[2:] + bits[1:2]


def kernel(
    n, height, width, ch,
    state, mask, k_one, target_hbm, k_two_hbm,
    pred_hbm, grad_one_hbm, grad_two_hbm,
    target, k_two, k_back, pred,
    x3, h3, e3, n3, xt, ht, slope, back,
    send_w, send_e, send_n, got_w, got_e, got_n, got_cw, got_ce,
    total, staged, landed, full,
    halo_send, halo_recv, sum_send, sum_recv, local_sem,
):
    me = lax.axis_index("lon")
    cells = height * width
    wide = 3 * ch
    step_rows = ROWS * width
    chunks = height // ROWS
    north_at = (height + 1) * width
    pad = total.shape[1]
    half = ch // 2
    orders = bit_orders(n)
    steps = len(orders[0])

    barrier = pltpu.get_barrier_semaphore()
    for k in range(1, n):
        pl.semaphore_signal(
            barrier, inc=1, device_id={"lon": lax.rem(me + k, n)}, device_id_type=MESH
        )
    load_target = pltpu.make_async_copy(target_hbm, target, local_sem.at[0])
    load_two = pltpu.make_async_copy(k_two_hbm, k_two, local_sem.at[1])
    load_two.start()
    load_target.start()

    flip = (
        lax.broadcasted_iota(jnp.int32, (width, width), 0)
        + lax.broadcasted_iota(jnp.int32, (width, width), 1)
        == width - 1
    ).astype(F32).astype(BF16)

    def mask_of(at, rows):
        m = mask[pl.ds(at, rows), :]
        return jnp.concatenate([m, m], axis=1)

    def send_halos(f):
        right, left = lax.rem(me + 1, n), lax.rem(me + n - 1, n)
        corner_w, corner_e = lax.rem(n - me, n), lax.rem(2 * n - 2 - me, n)

        def remote(src, dst, k, to):
            return pltpu.make_async_remote_copy(
                src_ref=src, dst_ref=dst, send_sem=halo_send.at[f, k], recv_sem=halo_recv.at[f, k],
                device_id={"lon": to}, device_id_type=MESH,
            )

        copies = [
            remote(send_e.at[f], got_w.at[f], 0, right),
            remote(send_w.at[f], got_e.at[f], 1, left),
            remote(send_n.at[f], got_n.at[f], 2, n - 1 - me),
        ]
        last = pl.ds(height - 8, 8)
        corners = [
            (remote(send_w.at[f, last], got_cw.at[f], 3, corner_w), corner_w, send_w, got_cw),
            (remote(send_e.at[f, last], got_ce.at[f], 4, corner_e), corner_e, send_e, got_ce),
        ]
        for copy in copies:
            copy.start()
        for copy, to, src, dst in corners:
            @pl.when(to != me)
            def _():
                copy.start()

            @pl.when(to == me)
            def _():
                dst[f] = src[f, last, :]

        def wait():
            for copy in copies:
                copy.wait()
            for copy, to, _, _ in corners:
                @pl.when(to != me)
                def _():
                    copy.wait()

        return wait

    def store_shifted(ref, at, values, rows):
        ref[pl.ds(at, rows), ch : 2 * ch] = values.astype(BF16)
        ref[pl.ds(at, rows), 0:ch] = pltpu.roll(values, 1, 0).astype(BF16)
        ref[pl.ds(at, rows), 2 * ch : wide] = pltpu.roll(values, rows - 1, 0).astype(BF16)

    tile_row = lax.broadcasted_iota(jnp.int32, (16, ch), 0)

    def patch(ref, f):
        def body(i, carry):
            first = pl.multiple_of((i + 1) * width, 16)
            last = pl.multiple_of((i + 2) * width - 16, 16)
            low = ref[pl.ds(first, 16), 0:ch].astype(F32)
            low = jnp.where(tile_row == 0, got_w[f, pl.ds(i, 1), :], low)
            ref[pl.ds(first, 16), 0:ch] = low.astype(BF16)
            high = ref[pl.ds(last, 16), 2 * ch : wide].astype(F32)
            high = jnp.where(tile_row == 15, got_e[f, pl.ds(i, 1), :], high)
            ref[pl.ds(last, 16), 2 * ch : wide] = high.astype(BF16)
            return carry

        lax.fori_loop(0, height, body, 0, unroll=8)

    row_at = lax.broadcasted_iota(jnp.int32, (width, ch), 0)

    def put_north(ref, at, f):
        row = got_n[f]
        ref[at : at + width, ch : 2 * ch] = row.astype(BF16)
        low = jnp.where(row_at == 0, got_cw[f, 7:8, :], pltpu.roll(row, 1, 0))
        high = jnp.where(row_at == width - 1, got_ce[f, 7:8, :], pltpu.roll(row, width - 1, 0))
        ref[at : at + width, 0:ch] = low.astype(BF16)
        ref[at : at + width, 2 * ch : wide] = high.astype(BF16)

    def edges(i, carry):
        first = pl.multiple_of(i * width, 16)
        last = pl.multiple_of((i + 1) * width - 16, 16)
        low = (state[pl.ds(first, 16), :] * mask_of(first, 16)).astype(F32)
        high = (state[pl.ds(last, 16), :] * mask_of(last, 16)).astype(F32)
        send_w[0, pl.ds(i, 1), :] = low[0:1, :]
        send_e[0, pl.ds(i, 1), :] = high[15:16, :]
        return carry

    lax.fori_loop(0, height, edges, 0, unroll=8)
    top = cells - width
    send_n[0] = jnp.dot(
        flip, state[top:cells, :] * mask_of(top, width), preferred_element_type=F32
    )
    pl.semaphore_wait(barrier, n - 1)
    wait_x = send_halos(0)

    for ref in (x3, h3, e3):
        ref[0:width, :] = jnp.zeros((width, wide), BF16)
    e3[north_at : north_at + width, :] = jnp.zeros((width, wide), BF16)
    back[0:width, :] = jnp.zeros((width, ch), BF16)
    back[north_at : north_at + width, :] = jnp.zeros((width, ch), BF16)
    if pad > 9 * ch:
        total[:, 9 * ch :, :] = jnp.zeros((2, pad - 9 * ch, ch), F32)

    def shift_state(c, carry):
        at = pl.multiple_of(c * step_rows, 16)
        values = (state[pl.ds(at, step_rows), :] * mask_of(at, step_rows)).astype(F32)
        store_shifted(x3, pl.multiple_of(at + width, 16), values, step_rows)
        return carry

    lax.fori_loop(0, chunks, shift_state, 0)

    load_two.wait()
    for a in range(3):
        for b in range(3):
            block = k_two[2 - a, (2 - b) * ch : (3 - b) * ch, :]
            k_back[a, b * ch : (b + 1) * ch, :] = block.T

    wait_x()
    patch(x3, 0)
    put_north(x3, north_at, 0)

    def conv(ref, weights, c):
        out = None
        for a in range(3):
            at = pl.multiple_of(c * step_rows + a * width, 16)
            term = jnp.dot(ref[pl.ds(at, step_rows), :], weights[a], preferred_element_type=F32)
            out = term if out is None else out + term
        return out

    def store_edges(f, c, values):
        for k in range(ROWS):
            i = c * ROWS + k
            send_w[f, pl.ds(i, 1), :] = values[k * width : k * width + 1, :]
            send_e[f, pl.ds(i, 1), :] = values[(k + 1) * width - 1 : (k + 1) * width, :]

    def layer_one(c, carry):
        at = pl.multiple_of(c * step_rows, 16)
        u = conv(x3, k_one, c).astype(BF16).astype(F32)
        m = mask_of(at, step_rows).astype(F32)
        cdf = 0.5 + 0.5 * lax.erf(u * (1.0 / math.sqrt(2.0)))
        density = jnp.exp(-0.5 * u * u) * (1.0 / math.sqrt(2.0 * math.pi))
        hidden = (u * cdf * m).astype(BF16).astype(F32)
        slope[pl.ds(at, step_rows), :] = (cdf + u * density) * m
        store_shifted(h3, pl.multiple_of(at + width, 16), hidden, step_rows)
        store_edges(1, c, hidden)
        return carry

    lax.fori_loop(0, chunks, layer_one, 0)
    send_n[1] = jnp.dot(flip, h3[cells : cells + width, ch : 2 * ch], preferred_element_type=F32)
    wait_h = send_halos(1)

    def transpose(ref, out):
        def body(c, carry):
            at = pl.multiple_of(c * step_rows, 128)
            for b in range(3):
                piece = ref[pl.ds(pl.multiple_of(at + width, 16), step_rows), b * ch : (b + 1) * ch]
                out[b * ch : (b + 1) * ch, pl.ds(at, step_rows)] = piece.T
            return carry

        lax.fori_loop(0, chunks, body, 0)
        out[:, cells : cells + width] = ref[north_at : north_at + width, :].T

    transpose(x3, xt)
    wait_h()
    patch(h3, 1)
    put_north(h3, north_at, 1)
    load_target.wait()
    scale = 1.0 / math.sqrt(cells * n)

    def layer_two(c, carry):
        at = pl.multiple_of(c * step_rows, 16)
        out = conv(h3, k_two, c)
        m = mask_of(at, step_rows).astype(F32)
        pred[pl.ds(at, step_rows), :] = (out * m).astype(BF16)
        error = m * (out - target[pl.ds(at, step_rows), :].astype(F32)) * scale
        error = error.astype(BF16).astype(F32)
        store_shifted(e3, pl.multiple_of(at + width, 16), error, step_rows)
        store_edges(2, c, error)
        return carry

    lax.fori_loop(0, chunks, layer_two, 0)
    send_n[2] = jnp.dot(flip, e3[cells : cells + width, ch : 2 * ch], preferred_element_type=F32)
    wait_e = send_halos(2)
    store_pred = pltpu.make_async_copy(pred, pred_hbm, local_sem.at[2])
    store_pred.start()

    def kernel_grad(g, a, field_t, error, lanes):
        depth = cells + (width if a == 2 else 0)
        at = (2 - a) * width
        total[g, a * wide : (a + 1) * wide, :] = jnp.dot(
            field_t[:, 0:depth], error[at : at + depth, lanes], preferred_element_type=F32
        )

    starts = [[0, 0], [0, 0]]
    flying = {}

    def partner(h, s):
        bit = 1 << orders[h][s]
        mine = lax.rem(me // bit, 2)
        return mine, me + (1 - 2 * mine) * bit

    def send_half(g, s):
        size = pad >> (s + 1)
        offset = pad - (pad >> s)
        for h in range(2):
            mine, to = partner(h, s)
            lanes = slice(h * half, (h + 1) * half)
            away = pl.multiple_of(starts[g][h] + (1 - mine) * size, 16)
            staged[g, h, offset : offset + size, :] = total[g, pl.ds(away, size), lanes].astype(BF16)
            copy = pltpu.make_async_remote_copy(
                src_ref=staged.at[g, h, pl.ds(offset, size)],
                dst_ref=landed.at[g, h, pl.ds(offset, size)],
                send_sem=sum_send.at[g, s, h], recv_sem=sum_recv.at[g, s, h],
                device_id={"lon": to}, device_id_type=MESH,
            )
            copy.start()
            flying[g, h] = copy
            starts[g][h] = starts[g][h] + mine * size

    def add_half(g, s):
        size = pad >> (s + 1)
        offset = pad - (pad >> s)
        for h in range(2):
            lanes = slice(h * half, (h + 1) * half)
            flying[g, h].wait()
            at = pl.ds(pl.multiple_of(starts[g][h], 16), size)
            total[g, at, lanes] = total[g, at, lanes] + landed[
                g, h, offset : offset + size, :
            ].astype(F32)

    def round_own(g):
        size = pad >> steps
        for h in range(2):
            lanes = slice(h * half, (h + 1) * half)
            at = pl.ds(pl.multiple_of(starts[g][h], 16), size)
            full[g, at, lanes] = total[g, at, lanes].astype(BF16)

    def send_own(g, s):
        size = pad >> (s + 1)
        for h in range(2):
            mine, to = partner(h, s)
            at = pl.ds(pl.multiple_of(starts[g][h], 16), size)
            own = full.at[g, at, pl.ds(h * half, half)]
            copy = pltpu.make_async_remote_copy(
                src_ref=own, dst_ref=own,
                send_sem=sum_send.at[g, 2 * steps - 1 - s, h],
                recv_sem=sum_recv.at[g, 2 * steps - 1 - s, h],
                device_id={"lon": to}, device_id_type=MESH,
            )
            copy.start()
            flying[g, h] = copy
            starts[g][h] = starts[g][h] - mine * size

    def wait_own(g):
        for h in range(2):
            flying[g, h].wait()

    def sum_stages(g):
        for s in range(steps):
            send_half(g, s)
            yield
            add_half(g, s)
        round_own(g)
        for s in reversed(range(steps)):
            send_own(g, s)
            yield
            wait_own(g)

    transpose(h3, ht)
    middle = slice(ch, 2 * ch)
    for a in range(3):
        kernel_grad(1, a, ht, e3, middle)
    sum_two = sum_stages(1)
    next(sum_two)

    wait_e()
    patch(e3, 2)
    put_north(n3, 0, 2)
    fold = None
    for b in range(3):
        term = jnp.dot(
            n3[:, b * ch : (b + 1) * ch], k_back[0, (2 - b) * ch : (3 - b) * ch, :],
            preferred_element_type=F32,
        )
        fold = term if fold is None else fold + term

    def pull_back(c, carry, extra=None):
        at = pl.multiple_of(c * step_rows, 16)
        grad = conv(e3, k_back, c)
        if extra is not None:
            grad = grad + extra
        grad = grad * slope[pl.ds(at, step_rows), :]
        back[pl.ds(pl.multiple_of(at + width, 16), step_rows), :] = grad.astype(BF16)
        return carry

    last = jnp.concatenate([jnp.zeros((step_rows - width, ch), F32), fold], axis=0)
    pull_back(chunks - 1, 0, last)
    groups = 3
    edges_at = [(chunks - 1) * k // groups for k in range(groups + 1)]
    for k in range(groups):
        lax.fori_loop(edges_at[k], edges_at[k + 1], pull_back, 0)
        next(sum_two)
    for a in range(3):
        kernel_grad(0, a, xt, back, slice(None))
        next(sum_two)
    sum_one = sum_stages(0)
    for _ in sum_one:
        next(sum_two, None)
    for _ in sum_two:
        pass
    stores = [
        pltpu.make_async_copy(full.at[0], grad_one_hbm, local_sem.at[3]),
        pltpu.make_async_copy(full.at[1], grad_two_hbm, local_sem.at[4]),
    ]
    for store in stores:
        store.start()
    store_pred.wait()
    for store in stores:
        store.wait()


def local(n, state_in, target, ocean_mask, kernel_one, kernel_two):
    height, width, ch = state_in.shape
    cells, wide = height * width, 3 * ch
    ext = (height + 2) * width
    pad = padded_rows(n, 9 * ch)
    steps = n.bit_length() - 1
    deep = -(-(cells + width) // 128) * 128
    mask = jnp.broadcast_to(
        ocean_mask.astype(BF16)[..., None], (height, width, ch // 2)
    ).reshape(cells, ch // 2)
    vmem, anywhere = pl.BlockSpec(memory_space=pltpu.VMEM), pl.BlockSpec(memory_space=pl.ANY)
    dma = pltpu.SemaphoreType.DMA
    prediction, grad_one, grad_two = pl.pallas_call(
        functools.partial(kernel, n, height, width, ch),
        out_shape=(
            jax.ShapeDtypeStruct((cells, ch), BF16),
            jax.ShapeDtypeStruct((pad, ch), BF16),
            jax.ShapeDtypeStruct((pad, ch), BF16),
        ),
        in_specs=[vmem, vmem, vmem, anywhere, anywhere],
        out_specs=(anywhere, anywhere, anywhere),
        scratch_shapes=[
            pltpu.VMEM((cells, ch), BF16),
            pltpu.VMEM((3, wide, ch), BF16),
            pltpu.VMEM((3, wide, ch), BF16),
            pltpu.VMEM((cells, ch), BF16),
            pltpu.VMEM((ext, wide), BF16),
            pltpu.VMEM((ext, wide), BF16),
            pltpu.VMEM((ext, wide), BF16),
            pltpu.VMEM((width, wide), BF16),
            pltpu.VMEM((wide, deep), BF16),
            pltpu.VMEM((wide, deep), BF16),
            pltpu.VMEM((cells, ch), F32),
            pltpu.VMEM((ext, ch), BF16),
            pltpu.VMEM((3, height, ch), F32),
            pltpu.VMEM((3, height, ch), F32),
            pltpu.VMEM((3, width, ch), F32),
            pltpu.VMEM((3, height, ch), F32),
            pltpu.VMEM((3, height, ch), F32),
            pltpu.VMEM((3, width, ch), F32),
            pltpu.VMEM((3, 8, ch), F32),
            pltpu.VMEM((3, 8, ch), F32),
            pltpu.VMEM((2, pad, ch), F32),
            pltpu.VMEM((2, 2, pad, ch // 2), BF16),
            pltpu.VMEM((2, 2, pad, ch // 2), BF16),
            pltpu.VMEM((2, pad, ch), BF16),
            dma((3, 5)),
            dma((3, 5)),
            dma((2, 2 * steps, 2)),
            dma((2, 2 * steps, 2)),
            dma((5,)),
        ],
        compiler_params=pltpu.CompilerParams(
            collective_id=0, has_side_effects=True, vmem_limit_bytes=60 * 1024 * 1024
        ),
        cost_estimate=pl.CostEstimate(
            flops=10 * cells * 9 * ch * ch, bytes_accessed=16 * cells * ch, transcendentals=2 * cells * ch
        ),
    )(
        state_in.reshape(cells, ch),
        mask,
        kernel_one.reshape(3, wide, ch),
        target.reshape(cells, ch),
        kernel_two.reshape(3, wide, ch),
    )
    shape = (3, 3, ch, ch)
    return (
        prediction.reshape(height, width, ch),
        grad_one[: 9 * ch].astype(F32).reshape(shape),
        grad_two[: 9 * ch].astype(F32).reshape(shape),
    )


def solution(mesh):
    return jax.shard_map(
        functools.partial(local, mesh.shape["lon"]),
        mesh=mesh,
        in_specs=(P("groups", "lon", None), P("groups", "lon", None), P("groups", "lon"), P(), P()),
        out_specs=(
            P("groups", "lon", None),
            P("groups", None, None, None),
            P("groups", None, None, None),
        ),
        check_vma=False,
    )
```

```python
import functools
import math

import jax
import jax.numpy as jnp
from jax import lax
from jax.experimental import pallas as pl
from jax.experimental.pallas import tpu as pltpu
from jax.sharding import PartitionSpec as P

F32, BF16 = jnp.float32, jnp.bfloat16
MESH = pl.DeviceIdType.MESH
ROWS = 8


def padded_rows(count, total):
    unit = 16 * count
    return -(-total // unit) * unit


def bit_orders(count):
    bits = list(range(count.bit_length() - 1))
    return bits, bits[:1] + bits[2:] + bits[1:2]


def kernel(
    n, height, width, ch,
    state, ocean, k_one_hbm, target_hbm, k_two_hbm,
    pred_hbm, grad_one_hbm, grad_two_hbm,
    mask, target, k_one, k_two, k_back, pred,
    x3, h3, e3, n3, xt, ht, slope, back,
    send_w, send_e, send_n, got_w, got_e, got_n, got_cw, got_ce,
    total, staged, landed, full,
    halo_send, halo_recv, sum_send, sum_recv, local_sem,
):
    me = lax.axis_index("lon")
    cells = height * width
    wide = 3 * ch
    step_rows = ROWS * width
    chunks = height // ROWS
    north_at = (height + 1) * width
    pad = total.shape[2]
    half = ch // 2
    orders = bit_orders(n)
    steps = len(orders[0])

    barrier = pltpu.get_barrier_semaphore()
    for k in range(1, n):
        pl.semaphore_signal(
            barrier, inc=1, device_id={"lon": lax.rem(me + k, n)}, device_id_type=MESH
        )
    load_target = pltpu.make_async_copy(target_hbm, target, local_sem.at[0])
    load_two = pltpu.make_async_copy(k_two_hbm, k_two, local_sem.at[1])
    load_one = pltpu.make_async_copy(k_one_hbm, k_one, local_sem.at[5])
    load_one.start()
    load_two.start()
    load_target.start()

    flip = (
        lax.broadcasted_iota(jnp.int32, (width, width), 0)
        + lax.broadcasted_iota(jnp.int32, (width, width), 1)
        == width - 1
    ).astype(F32).astype(BF16)

    def mask_of(at, rows):
        m = mask[pl.ds(at, rows), :]
        return jnp.concatenate([m, m], axis=1)

    eye = (
        lax.broadcasted_iota(jnp.int32, (width, width), 0)
        == lax.broadcasted_iota(jnp.int32, (width, width), 1)
    ).astype(F32)
    eyes = jnp.concatenate([eye] * ROWS, axis=0)
    cell_at = lax.broadcasted_iota(jnp.int32, (step_rows, ROWS), 0)
    row_of = lax.broadcasted_iota(jnp.int32, (step_rows, ROWS), 1) * width
    pick = ((cell_at >= row_of) & (cell_at < row_of + width)).astype(F32)
    for c in range(chunks):
        part = ocean[c * ROWS : (c + 1) * ROWS, :].astype(F32)
        part = jnp.dot(pick, part, preferred_element_type=F32) * eyes
        part = jnp.dot(part, jnp.ones((width, half), F32), preferred_element_type=F32)
        mask[c * step_rows : (c + 1) * step_rows, :] = part.astype(BF16)

    def send_halos(f, q, lo, hi):
        north = hi == height
        right, left = lax.rem(me + 1, n), lax.rem(me + n - 1, n)
        corner_w, corner_e = lax.rem(n - me, n), lax.rem(2 * n - 2 - me, n)

        def remote(src, dst, k, to):
            return pltpu.make_async_remote_copy(
                src_ref=src, dst_ref=dst, send_sem=halo_send.at[q, k], recv_sem=halo_recv.at[q, k],
                device_id={"lon": to}, device_id_type=MESH,
            )

        span = pl.ds(lo, hi - lo)
        copies = [
            remote(send_e.at[f, span], got_w.at[f, span], 0, right),
            remote(send_w.at[f, span], got_e.at[f, span], 1, left),
        ]
        if north:
            copies.append(remote(send_n.at[f], got_n.at[f], 2, n - 1 - me))
        last = pl.ds(height - 8, 8)
        corners = [
            (remote(send_w.at[f, last], got_cw.at[f], 3, corner_w), corner_w, send_w, got_cw),
            (remote(send_e.at[f, last], got_ce.at[f], 4, corner_e), corner_e, send_e, got_ce),
        ] if north else []
        for copy in copies:
            copy.start()
        for copy, to, src, dst in corners:
            @pl.when(to != me)
            def _():
                copy.start()

            @pl.when(to == me)
            def _():
                dst[f] = src[f, last, :]

        def wait():
            for copy in copies:
                copy.wait()
            for copy, to, _, _ in corners:
                @pl.when(to != me)
                def _():
                    copy.wait()

        return wait

    def store_shifted(ref, at, values, rows):
        ref[pl.ds(at, rows), ch : 2 * ch] = values.astype(BF16)
        ref[pl.ds(at, rows), 0:ch] = pltpu.roll(values, 1, 0).astype(BF16)
        ref[pl.ds(at, rows), 2 * ch : wide] = pltpu.roll(values, rows - 1, 0).astype(BF16)

    tile_row = lax.broadcasted_iota(jnp.int32, (16, ch), 0)

    def patch(ref, f, lo, hi):
        def body(i, carry):
            first = pl.multiple_of((i + 1) * width, 16)
            last = pl.multiple_of((i + 2) * width - 16, 16)
            low = ref[pl.ds(first, 16), 0:ch].astype(F32)
            low = jnp.where(tile_row == 0, got_w[f, pl.ds(i, 1), :], low)
            ref[pl.ds(first, 16), 0:ch] = low.astype(BF16)
            high = ref[pl.ds(last, 16), 2 * ch : wide].astype(F32)
            high = jnp.where(tile_row == 15, got_e[f, pl.ds(i, 1), :], high)
            ref[pl.ds(last, 16), 2 * ch : wide] = high.astype(BF16)
            return carry

        lax.fori_loop(lo, hi, body, 0, unroll=8)

    row_at = lax.broadcasted_iota(jnp.int32, (width, ch), 0)

    def put_north(ref, at, f):
        row = got_n[f]
        ref[at : at + width, ch : 2 * ch] = row.astype(BF16)
        low = jnp.where(row_at == 0, got_cw[f, 7:8, :], pltpu.roll(row, 1, 0))
        high = jnp.where(row_at == width - 1, got_ce[f, 7:8, :], pltpu.roll(row, width - 1, 0))
        ref[at : at + width, 0:ch] = low.astype(BF16)
        ref[at : at + width, 2 * ch : wide] = high.astype(BF16)

    def edges(i, carry):
        first = pl.multiple_of(i * width, 16)
        last = pl.multiple_of((i + 1) * width - 16, 16)
        low = (state[pl.ds(first, 16), :] * mask_of(first, 16)).astype(F32)
        high = (state[pl.ds(last, 16), :] * mask_of(last, 16)).astype(F32)
        send_w[0, pl.ds(i, 1), :] = low[0:1, :]
        send_e[0, pl.ds(i, 1), :] = high[15:16, :]
        return carry

    lax.fori_loop(0, height, edges, 0, unroll=8)
    top = cells - width
    send_n[0] = jnp.dot(
        flip, state[top:cells, :] * mask_of(top, width), preferred_element_type=F32
    )
    pl.semaphore_wait(barrier, n - 1)
    wait_x = send_halos(0, 0, 0, height)

    for ref in (x3, h3, e3):
        ref[0:width, :] = jnp.zeros((width, wide), BF16)
    e3[north_at : north_at + width, :] = jnp.zeros((width, wide), BF16)
    back[0:width, :] = jnp.zeros((width, ch), BF16)
    back[north_at : north_at + width, :] = jnp.zeros((width, ch), BF16)
    if pad > wide:
        total[:, :, wide:, :] = jnp.zeros((2, 3, pad - wide, ch), F32)

    def shift_state(c, carry):
        at = pl.multiple_of(c * step_rows, 16)
        values = (state[pl.ds(at, step_rows), :] * mask_of(at, step_rows)).astype(F32)
        store_shifted(x3, pl.multiple_of(at + width, 16), values, step_rows)
        return carry

    lax.fori_loop(0, chunks, shift_state, 0)

    load_two.wait()
    for a in range(3):
        for b in range(3):
            block = k_two[2 - a, (2 - b) * ch : (3 - b) * ch, :]
            k_back[a, b * ch : (b + 1) * ch, :] = block.T

    wait_x()
    patch(x3, 0, 0, height)
    put_north(x3, north_at, 0)
    load_one.wait()

    def conv(ref, weights, c):
        out = None
        for a in range(3):
            at = c * step_rows + a * width
            term = jnp.dot(ref[at : at + step_rows, :], weights[a], preferred_element_type=F32)
            out = term if out is None else out + term
        return out

    def store_edges(f, c, values):
        for k in range(ROWS):
            i = c * ROWS + k
            send_w[f, i : i + 1, :] = values[k * width : k * width + 1, :]
            send_e[f, i : i + 1, :] = values[(k + 1) * width - 1 : (k + 1) * width, :]

    def transpose(ref, out, c):
        at = c * step_rows
        for b in range(3):
            piece = ref[at + width : at + width + step_rows, b * ch : (b + 1) * ch]
            out[b * ch : (b + 1) * ch, at : at + step_rows] = piece.T

    def transpose_north(ref, out):
        out[:, cells : cells + width] = ref[north_at : north_at + width, :].T

    def layer_one(c):
        at = c * step_rows
        u = conv(x3, k_one, c).astype(BF16).astype(F32)
        transpose(x3, xt, c)
        m = mask_of(at, step_rows).astype(F32)
        cdf = 0.5 + 0.5 * lax.erf(u * (1.0 / math.sqrt(2.0)))
        density = jnp.exp(-0.5 * u * u) * (1.0 / math.sqrt(2.0 * math.pi))
        hidden = (u * cdf * m).astype(BF16).astype(F32)
        slope[at : at + step_rows, :] = (cdf + u * density) * m
        store_shifted(h3, at + width, hidden, step_rows)
        store_edges(1, c, hidden)

    split = chunks // 2
    for c in range(split):
        layer_one(c)
    wait_low = send_halos(1, 1, 0, split * ROWS)
    for c in range(split, chunks):
        layer_one(c)
    send_n[1] = jnp.dot(flip, h3[cells : cells + width, ch : 2 * ch], preferred_element_type=F32)
    wait_high = send_halos(1, 3, split * ROWS, height)
    transpose_north(x3, xt)
    scale = 1.0 / math.sqrt(cells * n)

    def layer_two(c):
        at = c * step_rows
        out = conv(h3, k_two, c)
        transpose(h3, ht, c)
        m = mask_of(at, step_rows).astype(F32)
        pred[at : at + step_rows, :] = (out * m).astype(BF16)
        error = m * (out - target[at : at + step_rows, :].astype(F32)) * scale
        error = error.astype(BF16).astype(F32)
        store_shifted(e3, at + width, error, step_rows)
        store_edges(2, c, error)

    load_target.wait()
    wait_low()
    patch(h3, 1, 0, split * ROWS)
    for c in range(split - 1):
        layer_two(c)
    wait_high()
    patch(h3, 1, split * ROWS, height)
    put_north(h3, north_at, 1)
    for c in range(split - 1, chunks):
        layer_two(c)
    send_n[2] = jnp.dot(flip, e3[cells : cells + width, ch : 2 * ch], preferred_element_type=F32)
    wait_e = send_halos(2, 2, 0, height)
    transpose_north(h3, ht)
    store_pred = pltpu.make_async_copy(pred, pred_hbm, local_sem.at[2])
    store_pred.start()

    def kernel_grad(g, a, field_t, error, lanes):
        depth = cells + (width if a == 2 else 0)
        at = (2 - a) * width
        total[g, a, 0:wide, :] = jnp.dot(
            field_t[:, 0:depth], error[at : at + depth, lanes], preferred_element_type=F32
        )

    def partner(h, s):
        bit = 1 << orders[h][s]
        mine = lax.rem(me // bit, 2)
        return mine, me + (1 - 2 * mine) * bit

    def sum_stages(g, p):
        starts = [0, 0]
        lanes = [slice(h * half, (h + 1) * half) for h in range(2)]
        for s in range(steps):
            size = pad >> (s + 1)
            offset = pad - (pad >> s)
            flying = []
            for h in range(2):
                mine, to = partner(h, s)
                away = pl.multiple_of(starts[h] + (1 - mine) * size, 16)
                staged[g, p, h, offset : offset + size, :] = total[
                    g, p, pl.ds(away, size), lanes[h]
                ].astype(BF16)
                copy = pltpu.make_async_remote_copy(
                    src_ref=staged.at[g, p, h, pl.ds(offset, size)],
                    dst_ref=landed.at[g, p, h, pl.ds(offset, size)],
                    send_sem=sum_send.at[g, p, s, h], recv_sem=sum_recv.at[g, p, s, h],
                    device_id={"lon": to}, device_id_type=MESH,
                )
                copy.start()
                flying.append(copy)
                starts[h] = starts[h] + mine * size
            yield
            for h in range(2):
                flying[h].wait()
                at = pl.ds(pl.multiple_of(starts[h], 16), size)
                total[g, p, at, lanes[h]] = total[g, p, at, lanes[h]] + landed[
                    g, p, h, offset : offset + size, :
                ].astype(F32)
        for h in range(2):
            at = pl.ds(pl.multiple_of(starts[h], 16), pad >> steps)
            full[g, p, at, lanes[h]] = total[g, p, at, lanes[h]].astype(BF16)
        for s in reversed(range(steps)):
            size = pad >> (s + 1)
            slot = 2 * steps - 1 - s
            flying = []
            for h in range(2):
                mine, to = partner(h, s)
                at = pl.ds(pl.multiple_of(starts[h], 16), size)
                own = full.at[g, p, at, pl.ds(h * half, half)]
                copy = pltpu.make_async_remote_copy(
                    src_ref=own, dst_ref=own,
                    send_sem=sum_send.at[g, p, slot, h], recv_sem=sum_recv.at[g, p, slot, h],
                    device_id={"lon": to}, device_id_type=MESH,
                )
                copy.start()
                flying.append(copy)
                starts[h] = starts[h] - mine * size
            yield
            for copy in flying:
                copy.wait()

    sums = []

    def advance():
        sums[:] = [one for one in sums if next(one, True) is None]

    middle = slice(ch, 2 * ch)
    for a in range(3):
        kernel_grad(1, a, ht, e3, middle)
        sums.append(sum_stages(1, a))
        advance()

    wait_e()
    patch(e3, 2, 0, height)
    put_north(n3, 0, 2)
    fold = None
    for b in range(3):
        term = jnp.dot(
            n3[:, b * ch : (b + 1) * ch], k_back[0, (2 - b) * ch : (3 - b) * ch, :],
            preferred_element_type=F32,
        )
        fold = term if fold is None else fold + term
    fold = jnp.concatenate([jnp.zeros((step_rows - width, ch), F32), fold], axis=0)

    for c in range(chunks):
        at = c * step_rows
        grad = conv(e3, k_back, c)
        if c == chunks - 1:
            grad = grad + fold
        grad = grad * slope[at : at + step_rows, :]
        back[at + width : at + width + step_rows, :] = grad.astype(BF16)
        if c in (chunks // 2 - 1, chunks - 1):
            advance()
    for a in range(3):
        kernel_grad(0, a, xt, back, slice(None))
        sums.append(sum_stages(0, a))
        advance()
    while sums:
        advance()
    stores = [
        pltpu.make_async_copy(full.at[0], grad_one_hbm, local_sem.at[3]),
        pltpu.make_async_copy(full.at[1], grad_two_hbm, local_sem.at[4]),
    ]
    for store in stores:
        store.start()
    store_pred.wait()
    for store in stores:
        store.wait()


def local(n, state_in, target, ocean_mask, kernel_one, kernel_two):
    height, width, ch = state_in.shape
    cells, wide = height * width, 3 * ch
    ext = (height + 2) * width
    pad = padded_rows(n, wide)
    steps = n.bit_length() - 1
    deep = -(-(cells + width) // 128) * 128
    vmem, anywhere = pl.BlockSpec(memory_space=pltpu.VMEM), pl.BlockSpec(memory_space=pl.ANY)
    dma = pltpu.SemaphoreType.DMA
    prediction, grad_one, grad_two = pl.pallas_call(
        functools.partial(kernel, n, height, width, ch),
        out_shape=(
            jax.ShapeDtypeStruct((cells, ch), BF16),
            jax.ShapeDtypeStruct((3, pad, ch), BF16),
            jax.ShapeDtypeStruct((3, pad, ch), BF16),
        ),
        in_specs=[vmem, vmem, anywhere, anywhere, anywhere],
        out_specs=(anywhere, anywhere, anywhere),
        scratch_shapes=[
            pltpu.VMEM((cells, ch // 2), BF16),
            pltpu.VMEM((cells, ch), BF16),
            pltpu.VMEM((3, wide, ch), BF16),
            pltpu.VMEM((3, wide, ch), BF16),
            pltpu.VMEM((3, wide, ch), BF16),
            pltpu.VMEM((cells, ch), BF16),
            pltpu.VMEM((ext, wide), BF16),
            pltpu.VMEM((ext, wide), BF16),
            pltpu.VMEM((ext, wide), BF16),
            pltpu.VMEM((width, wide), BF16),
            pltpu.VMEM((wide, deep), BF16),
            pltpu.VMEM((wide, deep), BF16),
            pltpu.VMEM((cells, ch), F32),
            pltpu.VMEM((ext, ch), BF16),
            pltpu.VMEM((3, height, ch), F32),
            pltpu.VMEM((3, height, ch), F32),
            pltpu.VMEM((3, width, ch), F32),
            pltpu.VMEM((3, height, ch), F32),
            pltpu.VMEM((3, height, ch), F32),
            pltpu.VMEM((3, width, ch), F32),
            pltpu.VMEM((3, 8, ch), F32),
            pltpu.VMEM((3, 8, ch), F32),
            pltpu.VMEM((2, 3, pad, ch), F32),
            pltpu.VMEM((2, 3, 2, pad, ch // 2), BF16),
            pltpu.VMEM((2, 3, 2, pad, ch // 2), BF16),
            pltpu.VMEM((2, 3, pad, ch), BF16),
            dma((4, 5)),
            dma((4, 5)),
            dma((2, 3, 2 * steps, 2)),
            dma((2, 3, 2 * steps, 2)),
            dma((6,)),
        ],
        compiler_params=pltpu.CompilerParams(
            collective_id=0, has_side_effects=True, vmem_limit_bytes=60 * 1024 * 1024
        ),
        cost_estimate=pl.CostEstimate(
            flops=10 * cells * 9 * ch * ch, bytes_accessed=16 * cells * ch, transcendentals=2 * cells * ch
        ),
    )(
        state_in.reshape(cells, ch),
        ocean_mask,
        kernel_one.reshape(3, wide, ch),
        target.reshape(cells, ch),
        kernel_two.reshape(3, wide, ch),
    )
    shape = (3, 3, ch, ch)
    return (
        prediction.reshape(height, width, ch),
        grad_one[:, :wide].astype(F32).reshape(shape),
        grad_two[:, :wide].astype(F32).reshape(shape),
    )


def solution(mesh):
    return jax.shard_map(
        functools.partial(local, mesh.shape["lon"]),
        mesh=mesh,
        in_specs=(P("groups", "lon", None), P("groups", "lon", None), P("groups", "lon"), P(), P()),
        out_specs=(
            P("groups", "lon", None),
            P("groups", None, None, None),
            P("groups", None, None, None),
        ),
        check_vma=False,
    )
```

```python
import functools
import math

import jax
import jax.numpy as jnp
from jax import lax
from jax.experimental import pallas as pl
from jax.experimental.pallas import tpu as pltpu
from jax.sharding import PartitionSpec as P

F32, BF16 = jnp.float32, jnp.bfloat16
MESH = pl.DeviceIdType.MESH
ROWS = 8


def padded_rows(count, total):
    unit = 16 * count
    return -(-total // unit) * unit


def stage_list(count, far_first):
    bits = count.bit_length() - 1
    radices = [2] * (bits - 2) + [4] if bits >= 3 else [2] * bits
    stages, stride = [], 1
    for radix in radices:
        stages.append((radix, stride))
        stride *= radix
    return stages[:1] + stages[:0:-1] if far_first else stages


def kernel(
    n, height, width, ch,
    state, ocean, k_one_hbm, target_hbm, k_two_hbm,
    pred_hbm, grad_one_hbm, grad_two_hbm,
    mask, target, k_one, k_two, k_back, pred,
    x3, h3, e3, n3, xt, ht, slope, back,
    send_w, send_e, send_n, got_w, got_e, got_n, got_cw, got_ce,
    total, staged, landed, full,
    halo_send, halo_recv, sum_send, sum_recv, local_sem, store_sem,
):
    me = lax.axis_index("lon")
    cells = height * width
    wide = 3 * ch
    step_rows = ROWS * width
    chunks = height // ROWS
    north_at = (height + 1) * width
    pad = total.shape[2]
    half = ch // 2

    barrier = pltpu.get_barrier_semaphore()
    for k in range(1, n):
        pl.semaphore_signal(
            barrier, inc=1, device_id={"lon": lax.rem(me + k, n)}, device_id_type=MESH
        )
    load_target = pltpu.make_async_copy(target_hbm, target, local_sem.at[0])
    load_two = pltpu.make_async_copy(k_two_hbm, k_two, local_sem.at[1])
    load_one = pltpu.make_async_copy(k_one_hbm, k_one, local_sem.at[5])
    load_one.start()
    load_two.start()
    load_target.start()

    flip = (
        lax.broadcasted_iota(jnp.int32, (width, width), 0)
        + lax.broadcasted_iota(jnp.int32, (width, width), 1)
        == width - 1
    ).astype(F32).astype(BF16)

    def mask_of(at, rows):
        m = mask[pl.ds(at, rows), :]
        return jnp.concatenate([m, m], axis=1)

    eye = (
        lax.broadcasted_iota(jnp.int32, (width, width), 0)
        == lax.broadcasted_iota(jnp.int32, (width, width), 1)
    ).astype(F32)
    eyes = jnp.concatenate([eye] * ROWS, axis=0)
    cell_at = lax.broadcasted_iota(jnp.int32, (step_rows, ROWS), 0)
    row_of = lax.broadcasted_iota(jnp.int32, (step_rows, ROWS), 1) * width
    pick = ((cell_at >= row_of) & (cell_at < row_of + width)).astype(F32)
    for c in range(chunks):
        part = ocean[c * ROWS : (c + 1) * ROWS, :].astype(F32)
        part = jnp.dot(pick, part, preferred_element_type=F32) * eyes
        part = jnp.dot(part, jnp.ones((width, half), F32), preferred_element_type=F32)
        mask[c * step_rows : (c + 1) * step_rows, :] = part.astype(BF16)

    def send_halos(f, q, lo, hi):
        north = hi == height
        right, left = lax.rem(me + 1, n), lax.rem(me + n - 1, n)
        corner_w, corner_e = lax.rem(n - me, n), lax.rem(2 * n - 2 - me, n)

        def remote(src, dst, k, to):
            return pltpu.make_async_remote_copy(
                src_ref=src, dst_ref=dst, send_sem=halo_send.at[q, k], recv_sem=halo_recv.at[q, k],
                device_id={"lon": to}, device_id_type=MESH,
            )

        span = pl.ds(lo, hi - lo)
        copies = [
            remote(send_e.at[f, span], got_w.at[f, span], 0, right),
            remote(send_w.at[f, span], got_e.at[f, span], 1, left),
        ]
        if north:
            copies.append(remote(send_n.at[f], got_n.at[f], 2, n - 1 - me))
        last = pl.ds(height - 8, 8)
        corners = [
            (remote(send_w.at[f, last], got_cw.at[f], 3, corner_w), corner_w, send_w, got_cw),
            (remote(send_e.at[f, last], got_ce.at[f], 4, corner_e), corner_e, send_e, got_ce),
        ] if north else []
        for copy in copies:
            copy.start()
        for copy, to, src, dst in corners:
            @pl.when(to != me)
            def _():
                copy.start()

            @pl.when(to == me)
            def _():
                dst[f] = src[f, last, :]

        def wait():
            for copy in copies:
                copy.wait()
            for copy, to, _, _ in corners:
                @pl.when(to != me)
                def _():
                    copy.wait()

        return wait

    def store_shifted(ref, at, values, rows):
        ref[pl.ds(at, rows), ch : 2 * ch] = values.astype(BF16)
        ref[pl.ds(at, rows), 0:ch] = pltpu.roll(values, 1, 0).astype(BF16)
        ref[pl.ds(at, rows), 2 * ch : wide] = pltpu.roll(values, rows - 1, 0).astype(BF16)

    tile_row = lax.broadcasted_iota(jnp.int32, (16, ch), 0)

    def patch(ref, f, lo, hi):
        def body(i, carry):
            first = pl.multiple_of((i + 1) * width, 16)
            last = pl.multiple_of((i + 2) * width - 16, 16)
            low = ref[pl.ds(first, 16), 0:ch].astype(F32)
            low = jnp.where(tile_row == 0, got_w[f, pl.ds(i, 1), :], low)
            ref[pl.ds(first, 16), 0:ch] = low.astype(BF16)
            high = ref[pl.ds(last, 16), 2 * ch : wide].astype(F32)
            high = jnp.where(tile_row == 15, got_e[f, pl.ds(i, 1), :], high)
            ref[pl.ds(last, 16), 2 * ch : wide] = high.astype(BF16)
            return carry

        lax.fori_loop(lo, hi, body, 0, unroll=8)

    row_at = lax.broadcasted_iota(jnp.int32, (width, ch), 0)

    def put_north(ref, at, f):
        row = got_n[f]
        ref[at : at + width, ch : 2 * ch] = row.astype(BF16)
        low = jnp.where(row_at == 0, got_cw[f, 7:8, :], pltpu.roll(row, 1, 0))
        high = jnp.where(row_at == width - 1, got_ce[f, 7:8, :], pltpu.roll(row, width - 1, 0))
        ref[at : at + width, 0:ch] = low.astype(BF16)
        ref[at : at + width, 2 * ch : wide] = high.astype(BF16)

    def edges(i, carry):
        first = pl.multiple_of(i * width, 16)
        last = pl.multiple_of((i + 1) * width - 16, 16)
        low = (state[pl.ds(first, 16), :] * mask_of(first, 16)).astype(F32)
        high = (state[pl.ds(last, 16), :] * mask_of(last, 16)).astype(F32)
        send_w[0, pl.ds(i, 1), :] = low[0:1, :]
        send_e[0, pl.ds(i, 1), :] = high[15:16, :]
        return carry

    lax.fori_loop(0, height, edges, 0, unroll=8)
    top = cells - width
    send_n[0] = jnp.dot(
        flip, state[top:cells, :] * mask_of(top, width), preferred_element_type=F32
    )
    pl.semaphore_wait(barrier, n - 1)
    wait_x = send_halos(0, 0, 0, height)

    for ref in (x3, h3, e3):
        ref[0:width, :] = jnp.zeros((width, wide), BF16)
    e3[north_at : north_at + width, :] = jnp.zeros((width, wide), BF16)
    back[0:width, :] = jnp.zeros((width, ch), BF16)
    back[north_at : north_at + width, :] = jnp.zeros((width, ch), BF16)
    if pad > wide:
        total[:, :, wide:, :] = jnp.zeros((2, 3, pad - wide, ch), F32)

    def shift_state(c, carry):
        at = pl.multiple_of(c * step_rows, 16)
        values = (state[pl.ds(at, step_rows), :] * mask_of(at, step_rows)).astype(F32)
        store_shifted(x3, pl.multiple_of(at + width, 16), values, step_rows)
        return carry

    lax.fori_loop(0, chunks, shift_state, 0)

    load_two.wait()
    for a in range(3):
        for b in range(3):
            block = k_two[2 - a, (2 - b) * ch : (3 - b) * ch, :]
            k_back[a, b * ch : (b + 1) * ch, :] = block.T

    wait_x()
    patch(x3, 0, 0, height)
    put_north(x3, north_at, 0)
    load_one.wait()

    def conv(ref, weights, c):
        out = None
        for a in range(3):
            at = c * step_rows + a * width
            term = jnp.dot(ref[at : at + step_rows, :], weights[a], preferred_element_type=F32)
            out = term if out is None else out + term
        return out

    def store_edges(f, c, values):
        for k in range(ROWS):
            i = c * ROWS + k
            send_w[f, i : i + 1, :] = values[k * width : k * width + 1, :]
            send_e[f, i : i + 1, :] = values[(k + 1) * width - 1 : (k + 1) * width, :]

    def transpose(ref, out, c):
        at = c * step_rows
        for b in range(3):
            piece = ref[at + width : at + width + step_rows, b * ch : (b + 1) * ch]
            out[b * ch : (b + 1) * ch, at : at + step_rows] = piece.T

    def transpose_north(ref, out):
        out[:, cells : cells + width] = ref[north_at : north_at + width, :].T

    def layer_one(c):
        at = c * step_rows
        u = conv(x3, k_one, c).astype(BF16).astype(F32)
        transpose(x3, xt, c)
        m = mask_of(at, step_rows).astype(F32)
        cdf = 0.5 + 0.5 * lax.erf(u * (1.0 / math.sqrt(2.0)))
        density = jnp.exp(-0.5 * u * u) * (1.0 / math.sqrt(2.0 * math.pi))
        hidden = (u * cdf * m).astype(BF16).astype(F32)
        slope[at : at + step_rows, :] = (cdf + u * density) * m
        store_shifted(h3, at + width, hidden, step_rows)
        store_edges(1, c, hidden)

    split = chunks // 2
    for c in range(split):
        layer_one(c)
    wait_low = send_halos(1, 1, 0, split * ROWS)
    for c in range(split, chunks):
        layer_one(c)
    send_n[1] = jnp.dot(flip, h3[cells : cells + width, ch : 2 * ch], preferred_element_type=F32)
    wait_high = send_halos(1, 3, split * ROWS, height)
    transpose_north(x3, xt)
    scale = 1.0 / math.sqrt(cells * n)

    def layer_two(c):
        at = c * step_rows
        out = conv(h3, k_two, c)
        transpose(h3, ht, c)
        m = mask_of(at, step_rows).astype(F32)
        pred[at : at + step_rows, :] = (out * m).astype(BF16)
        error = m * (out - target[at : at + step_rows, :].astype(F32)) * scale
        error = error.astype(BF16).astype(F32)
        store_shifted(e3, at + width, error, step_rows)
        store_edges(2, c, error)

    load_target.wait()
    wait_low()
    patch(h3, 1, 0, split * ROWS)
    for c in range(split - 1):
        layer_two(c)
    wait_high()
    patch(h3, 1, split * ROWS, height)
    put_north(h3, north_at, 1)
    for c in range(split - 1, chunks):
        layer_two(c)
    send_n[2] = jnp.dot(flip, e3[cells : cells + width, ch : 2 * ch], preferred_element_type=F32)
    wait_e = send_halos(2, 2, 0, height)
    transpose_north(h3, ht)
    store_pred = pltpu.make_async_copy(pred, pred_hbm, local_sem.at[2])
    store_pred.start()

    def kernel_grad(g, a, field_t, error, lanes):
        depth = cells + (width if a == 2 else 0)
        at = (2 - a) * width
        total[g, a, 0:wide, :] = jnp.dot(
            field_t[:, 0:depth], error[at : at + depth, lanes], preferred_element_type=F32
        )

    def sum_stages(g, p):
        stages = stage_list(n, g == 1 and p == 0)
        start, size, offset = 0, pad, 0
        others = []
        for s, (radix, stride) in enumerate(stages):
            digit = lax.rem(me // stride, radix)
            size //= radix
            flying = []
            for o in range(1, radix):
                j = lax.rem(digit + o, radix)
                away = pl.multiple_of(start + j * size, 16)
                spot = pl.ds(offset + (o - 1) * size, size)
                staged[g, p, spot, :] = total[g, p, pl.ds(away, size), :].astype(BF16)
                copy = pltpu.make_async_remote_copy(
                    src_ref=staged.at[g, p, spot], dst_ref=landed.at[g, p, spot],
                    send_sem=sum_send.at[g, p, s, o - 1], recv_sem=sum_recv.at[g, p, s, o - 1],
                    device_id={"lon": me + (j - digit) * stride}, device_id_type=MESH,
                )
                copy.start()
                flying.append((copy, spot))
            start = start + digit * size
            yield
            at = pl.ds(pl.multiple_of(start, 16), size)
            own = total[g, p, at, :]
            for copy, spot in flying:
                copy.wait()
                own = own + landed[g, p, spot, :].astype(F32)
            if s + 1 < len(stages):
                total[g, p, at, :] = own
            else:
                full[g, p, at, :] = own.astype(BF16)
            offset += (radix - 1) * size
        for s, (radix, stride) in reversed(list(enumerate(stages))):
            digit = lax.rem(me // stride, radix)
            slot = 2 * len(stages) - 1 - s
            own = full.at[g, p, pl.ds(pl.multiple_of(start, 16), size)]
            flying = []
            for o in range(1, radix):
                j = lax.rem(digit + o, radix)
                copy = pltpu.make_async_remote_copy(
                    src_ref=own, dst_ref=own,
                    send_sem=sum_send.at[g, p, slot, o - 1], recv_sem=sum_recv.at[g, p, slot, o - 1],
                    device_id={"lon": me + (j - digit) * stride}, device_id_type=MESH,
                )
                copy.start()
                flying.append(copy)
            start = start - digit * size
            size *= radix
            yield
            for copy in flying:
                copy.wait()
        store = pltpu.make_async_copy(
            full.at[g, p], (grad_two_hbm if g else grad_one_hbm).at[p], store_sem.at[g, p]
        )
        store.start()
        stores.append(store)

    stores = []
    sums = []

    def advance():
        sums[:] = [one for one in sums if next(one, True) is None]

    middle = slice(ch, 2 * ch)
    for a in range(3):
        kernel_grad(1, a, ht, e3, middle)
        sums.append(sum_stages(1, a))
        advance()

    wait_e()
    patch(e3, 2, 0, height)
    put_north(n3, 0, 2)
    fold = None
    for b in range(3):
        term = jnp.dot(
            n3[:, b * ch : (b + 1) * ch], k_back[0, (2 - b) * ch : (3 - b) * ch, :],
            preferred_element_type=F32,
        )
        fold = term if fold is None else fold + term
    fold = jnp.concatenate([jnp.zeros((step_rows - width, ch), F32), fold], axis=0)

    for c in range(chunks):
        at = c * step_rows
        grad = conv(e3, k_back, c)
        if c == chunks - 1:
            grad = grad + fold
        grad = grad * slope[at : at + step_rows, :]
        back[at + width : at + width + step_rows, :] = grad.astype(BF16)
        if c in (chunks // 2 - 1, chunks - 1):
            advance()
    for a in range(3):
        kernel_grad(0, a, xt, back, slice(None))
        sums.append(sum_stages(0, a))
        advance()
    while sums:
        advance()
    store_pred.wait()
    for store in stores:
        store.wait()


def local(n, state_in, target, ocean_mask, kernel_one, kernel_two):
    height, width, ch = state_in.shape
    cells, wide = height * width, 3 * ch
    ext = (height + 2) * width
    pad = padded_rows(n, wide)
    steps = len(stage_list(n, False))
    deep = -(-(cells + width) // 128) * 128
    vmem, anywhere = pl.BlockSpec(memory_space=pltpu.VMEM), pl.BlockSpec(memory_space=pl.ANY)
    dma = pltpu.SemaphoreType.DMA
    prediction, grad_one, grad_two = pl.pallas_call(
        functools.partial(kernel, n, height, width, ch),
        out_shape=(
            jax.ShapeDtypeStruct((cells, ch), BF16),
            jax.ShapeDtypeStruct((3, pad, ch), BF16),
            jax.ShapeDtypeStruct((3, pad, ch), BF16),
        ),
        in_specs=[vmem, vmem, anywhere, anywhere, anywhere],
        out_specs=(anywhere, anywhere, anywhere),
        scratch_shapes=[
            pltpu.VMEM((cells, ch // 2), BF16),
            pltpu.VMEM((cells, ch), BF16),
            pltpu.VMEM((3, wide, ch), BF16),
            pltpu.VMEM((3, wide, ch), BF16),
            pltpu.VMEM((3, wide, ch), BF16),
            pltpu.VMEM((cells, ch), BF16),
            pltpu.VMEM((ext, wide), BF16),
            pltpu.VMEM((ext, wide), BF16),
            pltpu.VMEM((ext, wide), BF16),
            pltpu.VMEM((width, wide), BF16),
            pltpu.VMEM((wide, deep), BF16),
            pltpu.VMEM((wide, deep), BF16),
            pltpu.VMEM((cells, ch), F32),
            pltpu.VMEM((ext, ch), BF16),
            pltpu.VMEM((3, height, ch), F32),
            pltpu.VMEM((3, height, ch), F32),
            pltpu.VMEM((3, width, ch), F32),
            pltpu.VMEM((3, height, ch), F32),
            pltpu.VMEM((3, height, ch), F32),
            pltpu.VMEM((3, width, ch), F32),
            pltpu.VMEM((3, 8, ch), F32),
            pltpu.VMEM((3, 8, ch), F32),
            pltpu.VMEM((2, 3, pad, ch), F32),
            pltpu.VMEM((2, 3, pad, ch), BF16),
            pltpu.VMEM((2, 3, pad, ch), BF16),
            pltpu.VMEM((2, 3, pad, ch), BF16),
            dma((4, 5)),
            dma((4, 5)),
            dma((2, 3, 2 * steps, 3)),
            dma((2, 3, 2 * steps, 3)),
            dma((6,)),
            dma((2, 3)),
        ],
        compiler_params=pltpu.CompilerParams(
            collective_id=0, has_side_effects=True, vmem_limit_bytes=60 * 1024 * 1024
        ),
        cost_estimate=pl.CostEstimate(
            flops=10 * cells * 9 * ch * ch, bytes_accessed=16 * cells * ch, transcendentals=2 * cells * ch
        ),
    )(
        state_in.reshape(cells, ch),
        ocean_mask,
        kernel_one.reshape(3, wide, ch),
        target.reshape(cells, ch),
        kernel_two.reshape(3, wide, ch),
    )
    shape = (3, 3, ch, ch)
    return (
        prediction.reshape(height, width, ch),
        grad_one[:, :wide].astype(F32).reshape(shape),
        grad_two[:, :wide].astype(F32).reshape(shape),
    )


def solution(mesh):
    return jax.shard_map(
        functools.partial(local, mesh.shape["lon"]),
        mesh=mesh,
        in_specs=(P("groups", "lon", None), P("groups", "lon", None), P("groups", "lon"), P(), P()),
        out_specs=(
            P("groups", "lon", None),
            P("groups", None, None, None),
            P("groups", None, None, None),
        ),
        check_vma=False,
    )
```
